32 devices in a mesh: rep: 4 (over y, x), shard: 8 (over z, core).
Axes of the slice: x: 2, y: 2, z: 4, core: 2. Of those that a mesh axis runs over, the one named last changes fastest.
Arguments:
- tokens: bfloat16 [32, 384, 768], P(('rep', 'shard')), may hold values from -6 to 6
- encoded: bfloat16 [32, 256, 768], P(('rep', 'shard')), may hold values from -6 to 6
- cotangent: bfloat16 [32, 384, 768], P(('rep', 'shard')), may hold values from -6 to 6
- buckets: int32 [384], replicated, may hold values from 0 to 31, as said below
- gains: bfloat16 [1, 3, 768], P(None, None, 'shard'), may hold values from 0.5 to 1.5
- self_query: bfloat16 [1, 768, 768], P(None, 'shard'), may hold values from -0.0546875 to 0.0546875
- self_kv: bfloat16 [1, 2, 768, 768], P(None, None, 'shard'), may hold values from -0.21875 to 0.21875
- self_out: bfloat16 [1, 768, 768], P(None, 'shard'), may hold values from -0.875 to 0.875
- cross_query: bfloat16 [1, 768, 768], P(None, 'shard'), may hold values from -0.0546875 to 0.0546875
- cross_kv: bfloat16 [1, 2, 768, 768], P(None, None, 'shard'), may hold values from -0.21875 to 0.21875
- cross_out: bfloat16 [1, 768, 768], P(None, 'shard'), may hold values from -0.875 to 0.875
- ffn_in: bfloat16 [1, 2, 768, 2048], P(None, None, 'shard'), may hold values from -0.21875 to 0.21875
- ffn_out: bfloat16 [1, 2048, 768], P(None, 'shard'), may hold values from -0.1875 to 0.1875
- bias_table: bfloat16 [32, 12], P('shard'), may hold values from -4 to 4
Outputs:
- layer_output: bfloat16 [32, 384, 768], P(('rep', 'shard'))
- grad_tokens: float32 [32, 384, 768], P(('rep', 'shard'))
- grad_encoded: float32 [32, 256, 768], P(('rep', 'shard'))
- grad_gains: float32 [1, 3, 768], P(None, None, 'shard')
- grad_self_query: float32 [1, 768, 768], P(None, 'shard')
- grad_self_kv: float32 [1, 2, 768, 768], P(None, None, 'shard')
- grad_self_out: float32 [1, 768, 768], P(None, 'shard')
- grad_cross_query: float32 [1, 768, 768], P(None, 'shard')
- grad_cross_kv: float32 [1, 2, 768, 768], P(None, None, 'shard')
- grad_cross_out: float32 [1, 768, 768], P(None, 'shard')
- grad_ffn_in: float32 [1, 2, 768, 2048], P(None, None, 'shard')
- grad_ffn_out: float32 [1, 2048, 768], P(None, 'shard')
- grad_bias_table: float32 [32, 12], P('shard')
The draws below stay inside these ranges and needn't reach their ends.
Inputs may be any that keep to these rules, and one draw needn't show every extreme that they name: `buckets`: never falls as the distance grows, equals the distance below 16, and is 31 at the distance 384 - 1.
All inputs are finite; a program needn't handle non-finite values.
Results may differ from the reference program's by a relative error of at most 0.023.
The reference program's roundings to bfloat16 on the way count: a program that leaves them out, or rounds other values in their place, can miss the bound.
Values may be sent and summed in bfloat16 or wider, within the bound.
A program may use at most 192 MiB of HBM per device.

```python
import jax
import jax.numpy as jnp
from jax import lax

D = 768
HEADS = 12
HEAD = 64
FF = 2048
NB = 32
LAYERS = 1
SEQ = 384
ENC = 256
SEQS = 32


def draw_buckets(key, part):
    key = jax.random.fold_in(key, 7)
    half = NB // 2
    order = jax.random.permutation(key, SEQ - half)
    breaks = jnp.sort(order[:NB - half - 1]) + half
    distance = jnp.arange(SEQ)
    above = jnp.sum((breaks[None, :] <= distance[:, None]).astype(jnp.int32), axis=1)
    return jnp.where(distance < half, distance, half + above).astype(jnp.int32)


def levels(own_key, extent, shards, smallest, largest):
    def one(dim, shards_of):
        heights = jax.random.uniform(jax.random.fold_in(jax.random.fold_in(own_key, 6), dim), (shards_of,), jnp.float32, smallest / len(shards), largest / len(shards))
        return jnp.repeat(jnp.exp(heights), extent[dim] // shards_of).reshape((-1,) + (1,) * (len(extent) - dim - 1))

    level = one(*shards[0])
    for cut in shards[1:]:
        level = level * one(*cut)
    return level


def noise(stream_key, dims, scale, limit, shards=(), kind=jnp.bfloat16):
    array = jax.random.normal(stream_key, dims, jnp.float32) * scale
    if len(shards) > 0:
        array = levels(stream_key, dims, shards, -0.22, 0.18) * array
    return jnp.clip(array, min=-limit, max=limit).astype(kind)


def setup_inputs(seed: int = 0) -> dict:
    splits = jax.random.split(jax.random.key(seed), 15)
    return {
        "tokens": noise(splits[0], (SEQS, SEQ, D), 1.0, 6.0, ((0, 32),)),
        "encoded": noise(splits[1], (SEQS, ENC, D), 1.0, 6.0, ((0, 32),)),
        "cotangent": noise(splits[2], (SEQS, SEQ, D), 1.0, 6.0, ((0, 32),)),
        "buckets": draw_buckets(jax.random.fold_in(splits[14], 71), 0),
        "gains": jnp.clip(1.0 + 0.1 * jax.random.normal(splits[4], (LAYERS, 3, D), jnp.float32), 0.5, 1.5).astype(jnp.bfloat16),
        "self_query": noise(splits[5], (LAYERS, D, D), (16 * D) ** -0.5, 0.0546875, ((1, 8),)),
        "self_kv": noise(splits[6], (LAYERS, 2, D, D), D ** -0.5, 0.21875, ((2, 8),)),
        "self_out": noise(splits[7], (LAYERS, D, D), (D // 16) ** -0.5, 0.875, ((1, 8),)),
        "cross_query": noise(splits[8], (LAYERS, D, D), (16 * D) ** -0.5, 0.0546875, ((1, 8),)),
        "cross_kv": noise(splits[9], (LAYERS, 2, D, D), D ** -0.5, 0.21875, ((2, 8),)),
        "cross_out": noise(splits[10], (LAYERS, D, D), (D // 16) ** -0.5, 0.875, ((1, 8),)),
        "ffn_in": noise(splits[11], (LAYERS, 2, D, FF), D ** -0.5, 0.21875, ((2, 8),)),
        "ffn_out": noise(splits[12], (LAYERS, FF, D), (FF // 2) ** -0.5, 0.1875, ((1, 8),)),
        "bias_table": noise(splits[13], (NB, HEADS), 1.0, 4.0, ((0, 8),)),
    }


@jax.custom_vjp
def low(v):
    return lax.optimization_barrier(v.astype(jnp.bfloat16)).astype(jnp.float32)

@jax.custom_vjp
def low_back(v):
    return v

def low_keep(v):
    return (low(v), None)

def low_pass(kept, grad):
    return (grad,)

def back_keep(v):
    return (v, None)

def back_low(kept, grad):
    return (low(grad),)
low.defvjp(low_keep, low_pass)
low_back.defvjp(back_keep, back_low)
negative = -1e+30
epsilon = 1e-06
highest = lax.Precision.HIGHEST
tanh_scale = 0.7978845608028654

def smooth_gate(value):
    return 0.5 * value * (1.0 + jnp.tanh(tanh_scale * (value + 0.044715 * value * value * value)))

def root_norm(rows, gain):
    return rows * lax.rsqrt(lax.optimization_barrier(jnp.mean(rows * rows, axis=-1, keepdims=True)) + epsilon) * gain

def product(left, right):
    return jnp.dot(left, right, precision=highest)

def split_heads(block):
    return block.reshape(block.shape[0], HEADS, HEAD)

def attend(query, keys, values, bias):
    raw = jnp.einsum('qhd,khd->hqk', split_heads(query), split_heads(keys), precision=highest)
    scores = low_back(raw) + bias
    top = lax.optimization_barrier(jnp.max(scores, axis=-1, keepdims=True))
    log_total = top + jnp.log(lax.optimization_barrier(jnp.sum(jnp.exp(scores - top), axis=-1, keepdims=True)))
    probs = low(jnp.exp(scores - log_total))
    mixed = jnp.einsum('hqk,khd->qhd', probs, split_heads(values), precision=highest)
    return low(low_back(mixed.reshape(query.shape)))

def layer(rows, context, weights, bias):
    gains, self_query, self_kv, self_out, cross_query, cross_kv, cross_out, ffn_in, ffn_out = weights
    normed = low(root_norm(rows, gains[0]))
    query = low(low_back(product(normed, self_query)))
    keys = low(low_back(product(normed, self_kv[0])))
    values = low(low_back(product(normed, self_kv[1])))
    rows = rows + low_back(product(attend(query, keys, values, bias), self_out))
    normed = low(root_norm(rows, gains[1]))
    query = low(low_back(product(normed, cross_query)))
    keys = low(low_back(product(context, cross_kv[0])))
    values = low(low_back(product(context, cross_kv[1])))
    rows = rows + low_back(product(attend(query, keys, values, 0.0), cross_out))
    normed = low(root_norm(rows, gains[2]))
    gate = low_back(product(normed, ffn_in[0]))
    up = low_back(product(normed, ffn_in[1]))
    hidden = low(smooth_gate(gate) * up)
    return rows + low_back(product(hidden, ffn_out))

def reference(tokens, encoded, cotangent, buckets, gains, self_query, self_kv, self_out, cross_query, cross_kv, cross_out, ffn_in, ffn_out, bias_table):
    distance = jnp.arange(SEQ)[:, None] - jnp.arange(SEQ)[None, :]
    bucket_grid = buckets[jnp.clip(distance, 0, SEQ - 1)]

    def forward(weights, table, inputs, states):
        bias = jnp.where(distance[None] >= 0, jnp.transpose(table[bucket_grid], (2, 0, 1)), negative)

        def one_sequence(pair):
            rows, context = pair
            for index in range(LAYERS):
                rows = layer(rows, context, tuple((item[index] for item in weights)), bias)
            return rows
        return lax.map(jax.checkpoint(one_sequence), (inputs, states))
    weights = tuple((item.astype(jnp.float32) for item in (gains, self_query, self_kv, self_out, cross_query, cross_kv, cross_out, ffn_in, ffn_out)))
    result, pull = jax.vjp(forward, weights, bias_table.astype(jnp.float32), tokens.astype(jnp.float32), encoded.astype(jnp.float32))
    grad_weights, grad_table, grad_tokens, grad_encoded = pull(cotangent.astype(jnp.float32))
    return (result.astype(jnp.bfloat16), grad_tokens, grad_encoded, grad_weights[0], grad_weights[1], grad_weights[2], grad_weights[3], grad_weights[4], grad_weights[5], grad_weights[6], grad_weights[7], grad_weights[8], grad_table)
```

```python
from functools import partial

import jax
import jax.numpy as jnp
from jax import lax
from jax.experimental import pallas as pl
from jax.experimental.pallas import tpu as pltpu
from jax.sharding import PartitionSpec as P

HEADS = 12
HEAD = 64
NB = 32
LAYERS = 1


negative = -1e30
epsilon = 1e-06
highest = lax.Precision.HIGHEST
tanh_scale = 0.7978845608028654


def smooth_gate(value):
    return 0.5 * value * (1.0 + jnp.tanh(tanh_scale * (value + 0.044715 * value * value * value)))


def gated(gate, up):
    return smooth_gate(gate) * up


def root_norm(rows, gain):
    return rows * lax.rsqrt(jnp.mean(rows * rows, axis=-1, keepdims=True) + epsilon) * gain


def product(left, right):
    return jnp.dot(left, right, preferred_element_type=jnp.float32)


def inner_rows(left, right):
    return lax.dot_general(
        left, right, (((0,), (0,)), ((), ())), preferred_element_type=jnp.float32
    )


def outer_rows(left, right):
    return lax.dot_general(
        left, right, (((1,), (1,)), ((), ())), preferred_element_type=jnp.float32
    )


STRIP = 128
PAIR = 2 * HEAD


def bias_of(line, length):
    extent = line.shape[-1]
    base = jnp.broadcast_to(line, (STRIP, extent))
    base = pltpu.roll(base, 0, 1, stride=1, stride_axis=0)
    strips = [base[:, :length]]
    for strip in range(1, length // STRIP):
        turn = strip * STRIP
        strips.append(
            jnp.concatenate([base[:, extent - turn :], base[:, : length - turn]], axis=1)
        )
    return jnp.concatenate(strips, axis=0)


def distance_sums(grid):
    length = grid.shape[-1]
    extent = 2 * length
    total = None
    for strip in range(length // STRIP):
        turn = strip * STRIP
        part = grid[turn : turn + STRIP, :]
        pieces = [jnp.zeros((STRIP, length - turn), jnp.float32), part]
        if turn:
            pieces.append(jnp.zeros((STRIP, turn), jnp.float32))
        part = jnp.concatenate(pieces, axis=1)
        total = part if total is None else total + part
    step = STRIP // 2
    while step >= 8:
        total = total[:step] + pltpu.roll(total[step:], extent - step, 1)
        step //= 2
    result = total[0:1]
    for row in range(1, 8):
        result = result + pltpu.roll(total, extent - row, 1)[row : row + 1]
    return result


def probabilities(query, keys, bias):
    scores = outer_rows(query, keys)
    if bias is not None:
        scores = scores + bias
    top = jnp.max(scores, axis=-1, keepdims=True)
    log_total = top + jnp.log(jnp.sum(jnp.exp(scores - top), axis=-1, keepdims=True))
    return jnp.exp(scores - log_total)


def forward_kernel(biased, query_ref, keys_ref, values_ref, *refs):
    for half in range(2):
        lanes = slice(half * HEAD, (half + 1) * HEAD)
        bias = bias_of(refs[0][half], query_ref.shape[0]) if biased else None
        probs = probabilities(query_ref[:, lanes], keys_ref[:, lanes], bias)
        mixed = product(probs.astype(jnp.bfloat16), values_ref[:, lanes])
        refs[-1][:, lanes] = mixed.astype(jnp.bfloat16)


def backward_kernel(biased, query_ref, keys_ref, values_ref, upstream_ref, *refs):
    outs = refs[1:] if biased else refs
    for half in range(2):
        lanes = slice(half * HEAD, (half + 1) * HEAD)
        query, keys = query_ref[:, lanes], keys_ref[:, lanes]
        values, upstream = values_ref[:, lanes], upstream_ref[:, lanes]
        bias = bias_of(refs[0][half], query.shape[0]) if biased else None
        probs = probabilities(query, keys, bias)
        outs[2][:, lanes] = inner_rows(probs.astype(jnp.bfloat16), upstream).astype(jnp.bfloat16)
        grad_probs = outer_rows(upstream, values)
        grad_scores = probs * (
            grad_probs - jnp.sum(probs * grad_probs, axis=-1, keepdims=True)
        )
        rounded = grad_scores.astype(jnp.bfloat16)
        outs[0][:, lanes] = product(rounded, keys).astype(jnp.bfloat16)
        outs[1][:, lanes] = inner_rows(rounded, query).astype(jnp.bfloat16)
        if biased:
            outs[3][0, half] = distance_sums(grad_scores)


def attention(kernel, operands, count, line=None):
    backward = len(operands) == 4
    rows = [item.shape[0] // count for item in operands]
    specs = [pl.BlockSpec((extent, PAIR), lambda s, h: (s, h)) for extent in rows]
    width = operands[0].shape[1]
    outs = [operands[i] for i in ((0, 1, 2) if backward else (0,))]
    out_shape = [jax.ShapeDtypeStruct(item.shape, jnp.bfloat16) for item in outs]
    out_specs = [
        pl.BlockSpec((item.shape[0] // count, PAIR), lambda s, h: (s, h)) for item in outs
    ]
    if line is not None:
        extent = line.shape[-1]
        operands = operands + (line,)
        specs.append(pl.BlockSpec((2, 1, extent), lambda s, h: (h, 0, 0)))
        if backward:
            out_shape.append(jax.ShapeDtypeStruct((count, HEADS, 1, extent), jnp.float32))
            out_specs.append(pl.BlockSpec((1, 2, 1, extent), lambda s, h: (s, h, 0, 0)))
    pairs = rows[0] * rows[1] * count
    return pl.pallas_call(
        partial(kernel, line is not None),
        grid=(count, width // PAIR),
        in_specs=specs,
        out_specs=out_specs,
        out_shape=out_shape,
        compiler_params=pltpu.CompilerParams(vmem_limit_bytes=32 * 1024 * 1024),
        cost_estimate=pl.CostEstimate(
            flops=2 * pairs * width * (5 if backward else 2),
            bytes_accessed=2 * width * sum(rows) * count * 2,
            transcendentals=2 * pairs * HEADS,
        ),
    )(*operands)


def bias_lines(table, buckets):
    length = buckets.shape[0]
    place = jnp.arange(2 * length)
    turned = jnp.concatenate(
        [buckets[:1], jnp.zeros((length,), buckets.dtype), buckets[:0:-1]]
    )
    onehot = (turned[:, None] == jnp.arange(NB)[None, :]).astype(jnp.float32)
    lines = jnp.einsum("ob,bh->ho", onehot, table.astype(jnp.float32), precision=highest)
    allowed = (place == 0) | (place > length)
    return jnp.where(allowed[None], lines, negative)[:, None, :]


def table_gradient(sums, buckets):
    length = buckets.shape[0]
    onehot = (buckets[::-1, None] == jnp.arange(NB)[None, :]).astype(jnp.float32)
    return jnp.einsum("ho,ob->bh", sums[:, 1 : length + 1], onehot, precision=highest)


def layer_forward(residual, encoded, weights, line):
    (
        gains,
        self_query,
        self_kv,
        self_out,
        cross_query,
        cross_kv,
        cross_out,
        ffn_in,
        ffn_out,
        table,
    ) = weights
    count = encoded.shape[0]
    width = residual.shape[1]
    enc_rows = encoded.reshape(-1, width)
    normed_self = root_norm(residual, gains[0].astype(jnp.float32)).astype(jnp.bfloat16)
    query = product(normed_self, self_query).astype(jnp.bfloat16)
    keys = product(normed_self, self_kv[0]).astype(jnp.bfloat16)
    values = product(normed_self, self_kv[1]).astype(jnp.bfloat16)
    (mixed,) = attention(forward_kernel, (query, keys, values), count, line)
    after_self = residual + product(mixed, self_out)
    normed_cross = root_norm(after_self, gains[1].astype(jnp.float32)).astype(jnp.bfloat16)
    cross_q = product(normed_cross, cross_query).astype(jnp.bfloat16)
    cross_k = product(enc_rows, cross_kv[0]).astype(jnp.bfloat16)
    cross_v = product(enc_rows, cross_kv[1]).astype(jnp.bfloat16)
    (cross_mixed,) = attention(forward_kernel, (cross_q, cross_k, cross_v), count)
    after_cross = after_self + product(cross_mixed, cross_out)
    normed_ffn = root_norm(after_cross, gains[2].astype(jnp.float32)).astype(jnp.bfloat16)
    gate = product(normed_ffn, ffn_in[0])
    up = product(normed_ffn, ffn_in[1])
    hidden = gated(gate, up).astype(jnp.bfloat16)
    output = after_cross + product(hidden, ffn_out)
    kept = (
        residual,
        after_self,
        after_cross,
        normed_self,
        query,
        keys,
        values,
        mixed,
        normed_cross,
        cross_q,
        cross_k,
        cross_v,
        cross_mixed,
        normed_ffn,
        gate,
        up,
        hidden,
    )
    return (output, kept)


def layer_backward(grad_rows, encoded, weights, line, kept, buckets):
    (
        gains,
        self_query,
        self_kv,
        self_out,
        cross_query,
        cross_kv,
        cross_out,
        ffn_in,
        ffn_out,
        table,
    ) = weights
    (
        residual,
        after_self,
        after_cross,
        normed_self,
        query,
        keys,
        values,
        mixed,
        normed_cross,
        cross_q,
        cross_k,
        cross_v,
        cross_mixed,
        normed_ffn,
        gate,
        up,
        hidden,
    ) = kept
    count = encoded.shape[0]
    width = grad_rows.shape[1]
    enc_rows = encoded.reshape(-1, width)
    branch = grad_rows.astype(jnp.bfloat16)
    grad_ffn_out = inner_rows(hidden, branch)
    unused, pull = jax.vjp(gated, gate, up)
    grad_gate, grad_up = pull(outer_rows(branch, ffn_out))
    grad_gate = grad_gate.astype(jnp.bfloat16)
    grad_up = grad_up.astype(jnp.bfloat16)
    grad_ffn_in = (inner_rows(normed_ffn, grad_gate), inner_rows(normed_ffn, grad_up))
    grad_normed = outer_rows(grad_gate, ffn_in[0]) + outer_rows(grad_up, ffn_in[1])
    unused, pull = jax.vjp(root_norm, after_cross, gains[2].astype(jnp.float32))
    grad_back, gain_ffn = pull(grad_normed)
    grad_rows = grad_rows + grad_back
    branch = grad_rows.astype(jnp.bfloat16)
    grad_cross_out = inner_rows(cross_mixed, branch)
    grad_mixed = outer_rows(branch, cross_out).astype(jnp.bfloat16)
    grad_cq, grad_ck, grad_cv = attention(
        backward_kernel, (cross_q, cross_k, cross_v, grad_mixed), count
    )
    grad_cross_query = inner_rows(normed_cross, grad_cq)
    grad_cross_kv = (inner_rows(enc_rows, grad_ck), inner_rows(enc_rows, grad_cv))
    grad_states = outer_rows(grad_ck, cross_kv[0]) + outer_rows(grad_cv, cross_kv[1])
    unused, pull = jax.vjp(root_norm, after_self, gains[1].astype(jnp.float32))
    grad_back, gain_cross = pull(outer_rows(grad_cq, cross_query))
    grad_rows = grad_rows + grad_back
    branch = grad_rows.astype(jnp.bfloat16)
    grad_self_out = inner_rows(mixed, branch)
    grad_mixed = outer_rows(branch, self_out).astype(jnp.bfloat16)
    grad_query, grad_keys, grad_values, sums = attention(
        backward_kernel, (query, keys, values, grad_mixed), count, line
    )
    grad_self_query = inner_rows(normed_self, grad_query)
    grad_self_kv = (
        inner_rows(normed_self, grad_keys),
        inner_rows(normed_self, grad_values),
    )
    grad_normed = (
        outer_rows(grad_query, self_query)
        + outer_rows(grad_keys, self_kv[0])
        + outer_rows(grad_values, self_kv[1])
    )
    unused, pull = jax.vjp(root_norm, residual, gains[0].astype(jnp.float32))
    grad_back, gain_self = pull(grad_normed)
    grad_rows = grad_rows + grad_back
    grad_table = table_gradient(jnp.sum(sums, axis=(0, 2)), buckets)
    grads = (
        jnp.stack([gain_self, gain_cross, gain_ffn]),
        grad_self_query,
        grad_self_kv,
        grad_self_out,
        grad_cross_query,
        grad_cross_kv,
        grad_cross_out,
        grad_ffn_in,
        grad_ffn_out,
        grad_table,
    )
    return (grad_rows, grad_states, grads)


def gather_square(stack):
    matrices, piece, width = stack.shape
    if lax.axis_size("rep") == matrices:
        own = lax.dynamic_index_in_dim(stack, lax.axis_index("rep"), 0, keepdims=False)
        whole = lax.all_gather(own, ("rep", "shard"), axis=0, tiled=True)
        return whole.reshape(matrices, -1, width)
    return lax.all_gather(stack, "shard", axis=1, tiled=True)


def gather_weights(
    gains, self_query, self_kv, self_out, cross_query, cross_kv, cross_out, ffn_in, ffn_out, table
):
    small = jnp.concatenate([gains[0].reshape(-1), table.reshape(-1)])
    small = lax.all_gather(small, "shard", axis=0)
    cut = gains[0].size
    all_gains = small[:, :cut].reshape(-1, 3, gains.shape[2]).transpose(1, 0, 2).reshape(3, -1)
    all_table = small[:, cut:].reshape(-1, table.shape[1])
    own = gather_square(jnp.concatenate([self_query, self_kv[0], self_out]))
    cross = gather_square(jnp.concatenate([cross_query, cross_kv[0], cross_out]))
    half = ffn_in.shape[3] // 2
    wide = gather_square(
        jnp.stack([ffn_in[0, m, :, h * half : (h + 1) * half] for m in (0, 1) for h in (0, 1)])
    )
    wide = (
        jnp.concatenate([wide[0], wide[1]], axis=1),
        jnp.concatenate([wide[2], wide[3]], axis=1),
    )
    deep = ffn_out[0].reshape(4, -1, ffn_out.shape[2])
    count = lax.axis_size("shard")
    deep = gather_square(deep)
    deep = deep.reshape(4, count, -1, ffn_out.shape[2]).transpose(1, 0, 2, 3)
    deep = deep.reshape(-1, ffn_out.shape[2])
    return (
        all_gains, own[0], own[1:3], own[3], cross[0], cross[1:3], cross[3], wide, deep, all_table,
    )


def scatter_sum(parts):
    stack = jnp.stack([part.astype(jnp.bfloat16) for part in parts])
    share = lax.psum_scatter(stack, "shard", scatter_dimension=1, tiled=True)
    return lax.psum(share, "rep").astype(jnp.float32)


def reduce_gradients(grads, gains_shape, table_shape):
    (gains, query, kv, out, cross_query, cross_kv, cross_out, ffn_in, ffn_out, table) = grads
    ffn_out = scatter_sum([ffn_out])
    ffn_in = scatter_sum(ffn_in)
    cross = scatter_sum([cross_query, cross_kv[0], cross_kv[1], cross_out])
    own = scatter_sum([query, kv[0], kv[1], out])
    small = lax.psum(
        jnp.concatenate([gains.reshape(-1), table.reshape(-1)]), ("rep", "shard")
    )
    place = lax.axis_index("shard")
    gains = small[: gains.size].reshape(gains.shape)
    table = small[gains.size :].reshape(table.shape)
    gains = lax.dynamic_slice_in_dim(gains, place * gains_shape[2], gains_shape[2], 1)
    table = lax.dynamic_slice_in_dim(table, place * table_shape[0], table_shape[0], 0)
    return (
        gains[None],
        own[0:1],
        own[1:3][None],
        own[3:4],
        cross[0:1],
        cross[1:3][None],
        cross[3:4],
        ffn_in[None],
        ffn_out,
        table,
    )


def shards(
    tokens,
    encoded,
    cotangent,
    buckets,
    gains,
    self_query,
    self_kv,
    self_out,
    cross_query,
    cross_kv,
    cross_out,
    ffn_in,
    ffn_out,
    bias_table,
):
    count, length, width = tokens.shape
    rows = tokens.reshape(-1, width).astype(jnp.float32)
    weights = gather_weights(
        gains, self_query, self_kv, self_out, cross_query, cross_kv, cross_out, ffn_in, ffn_out,
        bias_table,
    )
    line = bias_lines(weights[9], buckets)
    rows, kept = layer_forward(rows, encoded, weights, line)
    grad_rows = cotangent.reshape(-1, width).astype(jnp.float32)
    grad_rows, grad_states, grads = layer_backward(
        grad_rows, encoded, weights, line, kept, buckets
    )
    return (
        rows.astype(jnp.bfloat16).reshape(tokens.shape),
        grad_rows.reshape(tokens.shape),
        grad_states.reshape(encoded.shape),
    ) + reduce_gradients(grads, gains.shape, bias_table.shape)


def solution(mesh):
    return jax.shard_map(
        shards,
        mesh=mesh,
        in_specs=(
            P(("rep", "shard"), None, None),
            P(("rep", "shard"), None, None),
            P(("rep", "shard"), None, None),
            P(),
            P(None, None, "shard"),
            P(None, "shard", None),
            P(None, None, "shard", None),
            P(None, "shard", None),
            P(None, "shard", None),
            P(None, None, "shard", None),
            P(None, "shard", None),
            P(None, None, "shard", None),
            P(None, "shard", None),
            P("shard", None),
        ),
        out_specs=(
            P(("rep", "shard"), None, None),
            P(("rep", "shard"), None, None),
            P(("rep", "shard"), None, None),
            P(None, None, "shard"),
            P(None, "shard", None),
            P(None, None, "shard", None),
            P(None, "shard", None),
            P(None, "shard", None),
            P(None, None, "shard", None),
            P(None, "shard", None),
            P(None, None, "shard", None),
            P(None, "shard", None),
            P("shard", None),
        ),
        check_vma=False,
    )
```

```python
from functools import partial

import jax
import jax.numpy as jnp
from jax import lax
from jax.experimental import pallas as pl
from jax.experimental.pallas import tpu as pltpu
from jax.sharding import PartitionSpec as P

HEADS = 12
HEAD = 64
NB = 32
LAYERS = 1


negative = -1e30
epsilon = 1e-06
highest = lax.Precision.HIGHEST
tanh_scale = 0.7978845608028654


def smooth_gate(value):
    return 0.5 * value * (1.0 + jnp.tanh(tanh_scale * (value + 0.044715 * value * value * value)))


def gated(gate, up):
    return smooth_gate(gate) * up


def root_norm(rows, gain):
    return rows * lax.rsqrt(jnp.mean(rows * rows, axis=-1, keepdims=True) + epsilon) * gain


def product(left, right):
    return jnp.dot(left, right, preferred_element_type=jnp.float32)


def inner_rows(left, right):
    return lax.dot_general(
        left, right, (((0,), (0,)), ((), ())), preferred_element_type=jnp.float32
    )


def outer_rows(left, right):
    return lax.dot_general(
        left, right, (((1,), (1,)), ((), ())), preferred_element_type=jnp.float32
    )


STRIP = 128
PAIR = 2 * HEAD


def bias_of(line, length):
    extent = line.shape[-1]
    base = jnp.broadcast_to(line, (STRIP, extent))
    base = pltpu.roll(base, 0, 1, stride=1, stride_axis=0)
    strips = [base[:, :length]]
    for strip in range(1, length // STRIP):
        turn = strip * STRIP
        strips.append(
            jnp.concatenate([base[:, extent - turn :], base[:, : length - turn]], axis=1)
        )
    return jnp.concatenate(strips, axis=0)


def distance_sums(grid):
    length = grid.shape[-1]
    extent = 2 * length
    total = None
    for strip in range(length // STRIP):
        turn = strip * STRIP
        part = grid[turn : turn + STRIP, :]
        pieces = [jnp.zeros((STRIP, length - turn), jnp.float32), part]
        if turn:
            pieces.append(jnp.zeros((STRIP, turn), jnp.float32))
        part = jnp.concatenate(pieces, axis=1)
        total = part if total is None else total + part
    step = STRIP // 2
    while step >= 8:
        total = total[:step] + pltpu.roll(total[step:], extent - step, 1)
        step //= 2
    result = total[0:1]
    for row in range(1, 8):
        result = result + pltpu.roll(total, extent - row, 1)[row : row + 1]
    return result


def probabilities(query, keys, bias):
    scores = outer_rows(query, keys)
    if bias is not None:
        scores = scores + bias
    top = jnp.max(scores, axis=-1, keepdims=True)
    log_total = top + jnp.log(jnp.sum(jnp.exp(scores - top), axis=-1, keepdims=True))
    return jnp.exp(scores - log_total)


def forward_kernel(biased, query_ref, keys_ref, values_ref, *refs):
    for half in range(2):
        lanes = slice(half * HEAD, (half + 1) * HEAD)
        bias = bias_of(refs[0][half], query_ref.shape[0]) if biased else None
        probs = probabilities(query_ref[:, lanes], keys_ref[:, lanes], bias)
        mixed = product(probs.astype(jnp.bfloat16), values_ref[:, lanes])
        refs[-1][:, lanes] = mixed.astype(jnp.bfloat16)


def backward_kernel(biased, query_ref, keys_ref, values_ref, upstream_ref, *refs):
    outs = refs[1:] if biased else refs
    for half in range(2):
        lanes = slice(half * HEAD, (half + 1) * HEAD)
        query, keys = query_ref[:, lanes], keys_ref[:, lanes]
        values, upstream = values_ref[:, lanes], upstream_ref[:, lanes]
        bias = bias_of(refs[0][half], query.shape[0]) if biased else None
        probs = probabilities(query, keys, bias)
        outs[2][:, lanes] = inner_rows(probs.astype(jnp.bfloat16), upstream).astype(jnp.bfloat16)
        grad_probs = outer_rows(upstream, values)
        grad_scores = probs * (
            grad_probs - jnp.sum(probs * grad_probs, axis=-1, keepdims=True)
        )
        rounded = grad_scores.astype(jnp.bfloat16)
        outs[0][:, lanes] = product(rounded, keys).astype(jnp.bfloat16)
        outs[1][:, lanes] = inner_rows(rounded, query).astype(jnp.bfloat16)
        if biased:
            outs[3][0, half] = distance_sums(grad_scores)


def attention(kernel, operands, count, line=None):
    backward = len(operands) == 4
    rows = [item.shape[0] // count for item in operands]
    specs = [pl.BlockSpec((extent, PAIR), lambda s, h: (s, h)) for extent in rows]
    width = operands[0].shape[1]
    outs = [operands[i] for i in ((0, 1, 2) if backward else (0,))]
    out_shape = [jax.ShapeDtypeStruct(item.shape, jnp.bfloat16) for item in outs]
    out_specs = [
        pl.BlockSpec((item.shape[0] // count, PAIR), lambda s, h: (s, h)) for item in outs
    ]
    if line is not None:
        extent = line.shape[-1]
        operands = operands + (line,)
        specs.append(pl.BlockSpec((2, 1, extent), lambda s, h: (h, 0, 0)))
        if backward:
            out_shape.append(jax.ShapeDtypeStruct((count, HEADS, 1, extent), jnp.float32))
            out_specs.append(pl.BlockSpec((1, 2, 1, extent), lambda s, h: (s, h, 0, 0)))
    pairs = rows[0] * rows[1] * count
    return pl.pallas_call(
        partial(kernel, line is not None),
        grid=(count, width // PAIR),
        in_specs=specs,
        out_specs=out_specs,
        out_shape=out_shape,
        compiler_params=pltpu.CompilerParams(vmem_limit_bytes=32 * 1024 * 1024),
        cost_estimate=pl.CostEstimate(
            flops=2 * pairs * width * (5 if backward else 2),
            bytes_accessed=2 * width * sum(rows) * count * 2,
            transcendentals=2 * pairs * HEADS,
        ),
    )(*operands)


def bias_lines(table, buckets):
    length = buckets.shape[0]
    place = jnp.arange(2 * length)
    turned = jnp.concatenate(
        [buckets[:1], jnp.zeros((length,), buckets.dtype), buckets[:0:-1]]
    )
    onehot = (turned[:, None] == jnp.arange(NB)[None, :]).astype(jnp.float32)
    lines = jnp.einsum("ob,bh->ho", onehot, table.astype(jnp.float32), precision=highest)
    allowed = (place == 0) | (place > length)
    return jnp.where(allowed[None], lines, negative)[:, None, :]


def table_gradient(sums, buckets):
    length = buckets.shape[0]
    onehot = (buckets[::-1, None] == jnp.arange(NB)[None, :]).astype(jnp.float32)
    return jnp.einsum("ho,ob->bh", sums[:, 1 : length + 1], onehot, precision=highest)


def layer_forward(residual, encoded, weights, line):
    (
        gains,
        self_query,
        self_kv,
        self_out,
        cross_query,
        cross_kv,
        cross_out,
        ffn_in,
        ffn_out,
        table,
    ) = weights
    count = encoded.shape[0]
    width = residual.shape[1]
    enc_rows = encoded.reshape(-1, width)
    normed_self = root_norm(residual, gains[0].astype(jnp.float32)).astype(jnp.bfloat16)
    query = product(normed_self, self_query).astype(jnp.bfloat16)
    keys = product(normed_self, self_kv[0]).astype(jnp.bfloat16)
    values = product(normed_self, self_kv[1]).astype(jnp.bfloat16)
    (mixed,) = attention(forward_kernel, (query, keys, values), count, line)
    after_self = residual + product(mixed, self_out)
    normed_cross = root_norm(after_self, gains[1].astype(jnp.float32)).astype(jnp.bfloat16)
    cross_q = product(normed_cross, cross_query).astype(jnp.bfloat16)
    cross_k = product(enc_rows, cross_kv[0]).astype(jnp.bfloat16)
    cross_v = product(enc_rows, cross_kv[1]).astype(jnp.bfloat16)
    (cross_mixed,) = attention(forward_kernel, (cross_q, cross_k, cross_v), count)
    after_cross = after_self + product(cross_mixed, cross_out)
    normed_ffn = root_norm(after_cross, gains[2].astype(jnp.float32)).astype(jnp.bfloat16)
    gate = product(normed_ffn, ffn_in[0])
    up = product(normed_ffn, ffn_in[1])
    hidden = gated(gate, up).astype(jnp.bfloat16)
    output = after_cross + product(hidden, ffn_out)
    kept = (
        residual,
        after_self,
        after_cross,
        normed_self,
        query,
        keys,
        values,
        mixed,
        normed_cross,
        cross_q,
        cross_k,
        cross_v,
        cross_mixed,
        normed_ffn,
        gate,
        up,
        hidden,
    )
    return (output, kept)


def layer_backward(grad_rows, encoded, weights, line, kept, buckets):
    (
        gains,
        self_query,
        self_kv,
        self_out,
        cross_query,
        cross_kv,
        cross_out,
        ffn_in,
        ffn_out,
        table,
    ) = weights
    (
        residual,
        after_self,
        after_cross,
        normed_self,
        query,
        keys,
        values,
        mixed,
        normed_cross,
        cross_q,
        cross_k,
        cross_v,
        cross_mixed,
        normed_ffn,
        gate,
        up,
        hidden,
    ) = kept
    count = encoded.shape[0]
    width = grad_rows.shape[1]
    enc_rows = encoded.reshape(-1, width)
    branch = grad_rows.astype(jnp.bfloat16)
    grad_ffn_out = inner_rows(hidden, branch)
    unused, pull = jax.vjp(gated, gate, up)
    grad_gate, grad_up = pull(outer_rows(branch, ffn_out))
    grad_gate = grad_gate.astype(jnp.bfloat16)
    grad_up = grad_up.astype(jnp.bfloat16)
    grad_ffn_in = (inner_rows(normed_ffn, grad_gate), inner_rows(normed_ffn, grad_up))
    grad_normed = outer_rows(grad_gate, ffn_in[0]) + outer_rows(grad_up, ffn_in[1])
    unused, pull = jax.vjp(root_norm, after_cross, gains[2].astype(jnp.float32))
    grad_back, gain_ffn = pull(grad_normed)
    grad_rows = grad_rows + grad_back
    branch = grad_rows.astype(jnp.bfloat16)
    grad_cross_out = inner_rows(cross_mixed, branch)
    grad_mixed = outer_rows(branch, cross_out).astype(jnp.bfloat16)
    grad_cq, grad_ck, grad_cv = attention(
        backward_kernel, (cross_q, cross_k, cross_v, grad_mixed), count
    )
    grad_cross_query = inner_rows(normed_cross, grad_cq)
    grad_cross_kv = (inner_rows(enc_rows, grad_ck), inner_rows(enc_rows, grad_cv))
    grad_states = outer_rows(grad_ck, cross_kv[0]) + outer_rows(grad_cv, cross_kv[1])
    unused, pull = jax.vjp(root_norm, after_self, gains[1].astype(jnp.float32))
    grad_back, gain_cross = pull(outer_rows(grad_cq, cross_query))
    grad_rows = grad_rows + grad_back
    branch = grad_rows.astype(jnp.bfloat16)
    grad_self_out = inner_rows(mixed, branch)
    grad_mixed = outer_rows(branch, self_out).astype(jnp.bfloat16)
    grad_query, grad_keys, grad_values, sums = attention(
        backward_kernel, (query, keys, values, grad_mixed), count, line
    )
    grad_self_query = inner_rows(normed_self, grad_query)
    grad_self_kv = (
        inner_rows(normed_self, grad_keys),
        inner_rows(normed_self, grad_values),
    )
    grad_normed = (
        outer_rows(grad_query, self_query)
        + outer_rows(grad_keys, self_kv[0])
        + outer_rows(grad_values, self_kv[1])
    )
    unused, pull = jax.vjp(root_norm, residual, gains[0].astype(jnp.float32))
    grad_back, gain_self = pull(grad_normed)
    grad_rows = grad_rows + grad_back
    grad_table = table_gradient(jnp.sum(sums, axis=(0, 2)), buckets)
    grads = (
        jnp.stack([gain_self, gain_cross, gain_ffn]),
        grad_self_query,
        grad_self_kv,
        grad_self_out,
        grad_cross_query,
        grad_cross_kv,
        grad_cross_out,
        grad_ffn_in,
        grad_ffn_out,
        grad_table,
    )
    return (grad_rows, grad_states, grads)


def gather_square(stack):
    matrices, piece, width = stack.shape
    if lax.axis_size("rep") == matrices:
        own = lax.dynamic_index_in_dim(stack, lax.axis_index("rep"), 0, keepdims=False)
        whole = lax.all_gather(own, ("rep", "shard"), axis=0, tiled=True)
        return whole.reshape(matrices, -1, width)
    return lax.all_gather(stack, "shard", axis=1, tiled=True)


def gather_weights(
    gains, self_query, self_kv, self_out, cross_query, cross_kv, cross_out, ffn_in, ffn_out, table
):
    width = self_query.shape[2]
    small = jnp.concatenate([gains[0].reshape(-1), table.reshape(-1)])
    small = jnp.pad(small, (0, 16 * width - small.size)).reshape(1, 16, width)
    own = jnp.concatenate([self_query, self_kv[0], self_out])
    cross = jnp.concatenate([cross_query, cross_kv[0], cross_out])
    half = ffn_in.shape[3] // 2
    rest = half - width
    folds = width // rest
    piece = ffn_in.shape[2]
    wide = [ffn_in[0, m, :, h * half : (h + 1) * half] for m in (0, 1) for h in (0, 1)]
    most = jnp.stack([item[:, :width] for item in wide])
    last = jnp.stack([item[:, width:] for item in wide]).reshape(4, folds, -1, rest)
    last = jnp.concatenate([last[:, fold] for fold in range(folds)], axis=2)
    deep = ffn_out[0].reshape(4, -1, width)
    blocks = [own, cross, most, last, deep, jnp.broadcast_to(small, (4, 16, width))]
    count = lax.axis_size("shard")
    every = gather_square(jnp.concatenate(blocks, axis=1)).reshape(4, count, -1, width)
    cuts, start = [], 0
    for block in blocks:
        cuts.append(every[:, :, start : start + block.shape[1]])
        start += block.shape[1]
    own = cuts[0].reshape(4, -1, width)
    cross = cuts[1].reshape(4, -1, width)
    last = jnp.concatenate(
        [cuts[3][..., fold * rest : (fold + 1) * rest] for fold in range(folds)], axis=2
    )
    wide = jnp.concatenate([cuts[2], last], axis=3).reshape(4, count * piece, half)
    wide = (
        jnp.concatenate([wide[0], wide[1]], axis=1),
        jnp.concatenate([wide[2], wide[3]], axis=1),
    )
    deep = cuts[4].transpose(1, 0, 2, 3).reshape(-1, width)
    small = cuts[5][0].reshape(count, -1)
    cut = gains[0].size
    all_gains = small[:, :cut].reshape(count, 3, -1).transpose(1, 0, 2).reshape(3, -1)
    all_table = small[:, cut : cut + table.size].reshape(-1, table.shape[1])
    return (
        all_gains, own[0], own[1:3], own[3], cross[0], cross[1:3], cross[3], wide, deep, all_table,
    )


def scatter_sum(parts):
    stack = jnp.stack([part.astype(jnp.bfloat16) for part in parts])
    share = lax.psum_scatter(stack, "shard", scatter_dimension=1, tiled=True)
    return lax.psum(share, "rep").astype(jnp.float32)


def reduce_gradients(grads, gains_shape, table_shape):
    (gains, query, kv, out, cross_query, cross_kv, cross_out, ffn_in, ffn_out, table) = grads
    ffn_out = scatter_sum([ffn_out])
    ffn_in = scatter_sum(ffn_in)
    cross = scatter_sum([cross_query, cross_kv[0], cross_kv[1], cross_out])
    own = scatter_sum([query, kv[0], kv[1], out])
    small = lax.psum(
        jnp.concatenate([gains.reshape(-1), table.reshape(-1)]), ("rep", "shard")
    )
    place = lax.axis_index("shard")
    gains = small[: gains.size].reshape(gains.shape)
    table = small[gains.size :].reshape(table.shape)
    gains = lax.dynamic_slice_in_dim(gains, place * gains_shape[2], gains_shape[2], 1)
    table = lax.dynamic_slice_in_dim(table, place * table_shape[0], table_shape[0], 0)
    return (
        gains[None],
        own[0:1],
        own[1:3][None],
        own[3:4],
        cross[0:1],
        cross[1:3][None],
        cross[3:4],
        ffn_in[None],
        ffn_out,
        table,
    )


def shards(
    tokens,
    encoded,
    cotangent,
    buckets,
    gains,
    self_query,
    self_kv,
    self_out,
    cross_query,
    cross_kv,
    cross_out,
    ffn_in,
    ffn_out,
    bias_table,
):
    count, length, width = tokens.shape
    rows = tokens.reshape(-1, width).astype(jnp.float32)
    weights = gather_weights(
        gains, self_query, self_kv, self_out, cross_query, cross_kv, cross_out, ffn_in, ffn_out,
        bias_table,
    )
    line = bias_lines(weights[9], buckets)
    rows, kept = layer_forward(rows, encoded, weights, line)
    grad_rows = cotangent.reshape(-1, width).astype(jnp.float32)
    grad_rows, grad_states, grads = layer_backward(
        grad_rows, encoded, weights, line, kept, buckets
    )
    return (
        rows.astype(jnp.bfloat16).reshape(tokens.shape),
        grad_rows.reshape(tokens.shape),
        grad_states.reshape(encoded.shape),
    ) + reduce_gradients(grads, gains.shape, bias_table.shape)


def solution(mesh):
    return jax.shard_map(
        shards,
        mesh=mesh,
        in_specs=(
            P(("rep", "shard"), None, None),
            P(("rep", "shard"), None, None),
            P(("rep", "shard"), None, None),
            P(),
            P(None, None, "shard"),
            P(None, "shard", None),
            P(None, None, "shard", None),
            P(None, "shard", None),
            P(None, "shard", None),
            P(None, None, "shard", None),
            P(None, "shard", None),
            P(None, None, "shard", None),
            P(None, "shard", None),
            P("shard", None),
        ),
        out_specs=(
            P(("rep", "shard"), None, None),
            P(("rep", "shard"), None, None),
            P(("rep", "shard"), None, None),
            P(None, None, "shard"),
            P(None, "shard", None),
            P(None, None, "shard", None),
            P(None, "shard", None),
            P(None, "shard", None),
            P(None, None, "shard", None),
            P(None, "shard", None),
            P(None, None, "shard", None),
            P(None, "shard", None),
            P("shard", None),
        ),
        check_vma=False,
    )
```
